32 devices in a mesh: scene: 2 (over y), aper: 8 (over z, x), range: 2 (over core).
Axes of the slice: x: 2, y: 2, z: 4, core: 2. Of those that a mesh axis runs over, the one named last changes fastest.
Arguments:
- images: bfloat16 [16, 2, 512, 256], P(('scene', 'aper'), None, None, 'range'), parts along dimension 0, may hold values from -6 to 6
- interp_matrix: bfloat16 [1024, 512], replicated, may hold values from -0.25 to 0.25
- offsets: int32 [3, 2, 1024], replicated, may hold values from -28 to 28, as said below
- tap_index: int32 [3, 2, 1024], replicated, may hold values from 0 to 15
- tap_table: float32 [16, 8], replicated, may hold values from -1.5 to 1.5
- phase_base: float32 [3, 2, 1024], replicated, may hold values from -3.140625 to 3.140625
- phase_slope: float32 [3, 2, 1024], replicated, may hold values from -0.5 to 0.5
Outputs:
- merged: bfloat16 [16, 2, 512, 256], P(('scene', 'aper'), None, None, 'range'), parts along dimension 0
The draws below stay inside these ranges and needn't reach their ends.
There are 2 independent parts, one for each index of `scene`. The reference program is written for one: setup_inputs(seed, part) draws one part's arguments, and reference() takes and returns one part's arrays. A program takes and returns all parts, laid end to end along the dimension named above; an argument that names none is the same for every part. Nothing has to cross between parts.
Inputs may be any that keep to these rules, and one draw needn't show every extreme that they name: `offsets`: for every level and role both -28 and 28 occur.
All inputs are finite; a program needn't handle non-finite values.
Results may differ from the reference program's by a relative error of at most 0.0085.
Values may be sent and summed in bfloat16 or wider, within the bound.
No kernel may reach another device: no remote copies, remote signals or barrier semaphores. Data moves between devices by JAX's collectives and lax.ppermute only.
A program may use at most 64 MiB of HBM per device.

```python
from functools import partial
import jax
import jax.numpy as jnp
from jax import lax

ANG = 512
LEVELS = 3
HALO = 32
MAXOFF = 28
NFRAC = 16
TAPS = 8
APERS = 8
RANGE = 256
PARENT = 1024


def draw_offsets(key, part):
    values = jax.random.randint(jax.random.fold_in(key, 17), (LEVELS, 2, PARENT), -MAXOFF, MAXOFF + 1, dtype=jnp.int32)
    values = values.at[:, :, 0].set(-MAXOFF)
    values = values.at[:, :, 1].set(MAXOFF)
    return values


def plant(values, rng, smallest, high):
    longest = values.shape.index(max(values.shape))
    spots = []
    for shift in (0, 1):
        where = [jax.random.randint(jax.random.fold_in(rng, axis), (), 0, length) for axis, length in enumerate(values.shape)]
        where[longest] = (where[longest] + shift) % values.shape[longest]
        spots.append(tuple(where))
    return values.at[spots[0]].set(smallest).at[spots[1]].set(high)


def levels(own_key, extent, pieces, low, high):
    def one(axis_at, parts):
        steps = jax.random.uniform(jax.random.fold_in(jax.random.fold_in(own_key, 6), axis_at), (parts,), jnp.float32, low / len(pieces), high / len(pieces))
        return jnp.repeat(jnp.exp(steps), extent[axis_at] // parts).reshape((-1,) + (1,) * (len(extent) - axis_at - 1))

    factor_of = one(*pieces[0])
    for cut in pieces[1:]:
        factor_of = factor_of * one(*cut)
    return factor_of


def scatter_about(stream_key, dims, deviation, bound, cuts=(), held_as=jnp.bfloat16):
    array = jax.random.normal(stream_key, dims, jnp.float32) * deviation
    if len(cuts) > 0:
        array = levels(stream_key, dims, cuts, -0.22, 0.18) * array
    return jnp.clip(array, min=-bound, max=bound).astype(held_as)


def setup_inputs(seed: int = 0, part: int = 0) -> dict:
    key_list = jax.random.split(jax.random.key(seed), 8)
    own_keys = jax.random.split(jax.random.fold_in(key_list[7], part), 8)
    images = scatter_about(own_keys[0], (APERS, 2, ANG, RANGE), 1.0, 6.0, ((0, 8), (3, 2)))
    interp_matrix = scatter_about(key_list[1], (PARENT, ANG), ANG ** -0.5, 0.25)
    offsets = draw_offsets(jax.random.fold_in(key_list[7], 71), part)
    tap_index = plant(jax.random.randint(key_list[3], (LEVELS, 2, PARENT), 0, NFRAC), jax.random.fold_in(key_list[3], 1), 0, NFRAC - 1).astype(jnp.int32)
    tap_table = scatter_about(key_list[4], (NFRAC, TAPS), 0.25, 1.5, (), jnp.float32)
    phase_base = jnp.clip(jax.random.uniform(key_list[5], (LEVELS, 2, PARENT), jnp.float32, -3.140625, 3.140625), -3.140625, 3.140625)
    phase_slope = jnp.clip(jax.random.uniform(key_list[6], (LEVELS, 2, PARENT), jnp.float32, -0.5, 0.5), -0.5, 0.5)
    return dict(images=images, interp_matrix=interp_matrix, offsets=offsets, tap_index=tap_index, tap_table=tap_table, phase_base=phase_base, phase_slope=phase_slope)


def shifted(inter, shift_rows, tap_rows, first_col, out_width):
    taps_count = tap_rows.shape[1]
    needed = out_width + taps_count - 1
    total_width = inter.shape[2]
    start_cols = (first_col - 3 + shift_rows).astype(jnp.int32)
    moved = inter
    for bit_number in range((total_width - needed).bit_length()):
        stride_len = 1 << bit_number
        rolled = jnp.concatenate([moved[:, :, stride_len:], jnp.zeros_like(moved[:, :, :stride_len])], axis=2)
        chosen_bits = ((start_cols >> bit_number) & 1) == 1
        moved = jnp.where(chosen_bits[None, :, None], rolled, moved)
    window = moved[:, :, :needed]
    summed = jnp.zeros(window.shape[:2] + (out_width,), jnp.float32)
    for tap_number in range(taps_count):
        summed = summed + tap_rows[None, :, tap_number, None] * window[:, :, tap_number:tap_number + out_width].astype(jnp.float32)
    return summed


def child_term(inter, merge_level, child_role, offsets, tap_index, tap_table, phase_base, phase_slope):
    padded = jnp.pad(inter, ((0, 0), (0, 0), (HALO, HALO)))
    onehot = (tap_index[merge_level, child_role][:, None] == jnp.arange(NFRAC, dtype=jnp.int32)[None, :]).astype(jnp.float32)
    tap_rows = jnp.dot(onehot, tap_table, precision=lax.Precision.HIGHEST, preferred_element_type=jnp.float32)
    summed = shifted(padded, offsets[merge_level, child_role], tap_rows, HALO, RANGE)
    positions = jnp.arange(RANGE).astype(jnp.float32)
    phase_angle = phase_base[merge_level, child_role][:, None] + phase_slope[merge_level, child_role][:, None] * positions[None, :]
    cosine = jnp.cos(phase_angle)
    sine_part = jnp.sin(phase_angle)
    real_part = summed[0]
    imag_part = summed[1]
    return jnp.stack([real_part * cosine - imag_part * sine_part, real_part * sine_part + imag_part * cosine])


def merge_pair(merge_level, interp_matrix, offsets, tap_index, tap_table, phase_base, phase_slope, children):
    summed = jnp.zeros((2, PARENT, RANGE), jnp.float32)
    for child_role in range(2):
        inter = jnp.einsum("pa,can->cpn", interp_matrix.astype(jnp.float32), children[child_role].astype(jnp.float32),
                           precision=lax.Precision.HIGHEST).astype(jnp.bfloat16)
        summed = summed + child_term(inter, merge_level, child_role, offsets, tap_index, tap_table, phase_base, phase_slope)
    parent = summed.astype(jnp.bfloat16)
    return jnp.stack([parent[:, :ANG], parent[:, ANG:]])


def reference(images, interp_matrix, offsets, tap_index, tap_table, phase_base, phase_slope):
    current = images
    for merge_level in range(LEVELS):
        lower = 2 ** merge_level
        upper = APERS // (2 * lower)
        grouped = current.reshape(upper, 2, lower, 2, ANG, RANGE)
        pairs = jnp.transpose(grouped, (0, 2, 1, 3, 4, 5)).reshape(upper * lower, 2, 2, ANG, RANGE)
        merged = lax.map(partial(merge_pair, merge_level, interp_matrix, offsets, tap_index, tap_table, phase_base, phase_slope), pairs)
        current = jnp.transpose(merged.reshape(upper, lower, 2, 2, ANG, RANGE), (0, 2, 1, 3, 4, 5)).reshape(APERS, 2, ANG, RANGE)
    return current
```

```python
import functools

import jax
import jax.numpy as jnp
from jax import lax
from jax.experimental import pallas as pl
from jax.experimental.pallas import tpu as pltpu
from jax.sharding import PartitionSpec as P

HALO = 32
LANES = 128
ROWS = 8
KERNEL_VMEM = 8 << 20
VMEM = pl.BlockSpec(memory_space=pltpu.VMEM)


def run(kernel, outs, args, scratch=(), flops=0):
    size = sum(o.size * o.dtype.itemsize for o in outs)
    return pl.pallas_call(
        kernel,
        out_shape=outs,
        in_specs=[VMEM] * len(args),
        out_specs=[VMEM] * len(outs),
        scratch_shapes=scratch,
        compiler_params=pltpu.CompilerParams(vmem_limit_bytes=KERNEL_VMEM),
        cost_estimate=pl.CostEstimate(flops=flops, bytes_accessed=size, transcendentals=0),
    )(*args)


def from_partner(value, axis, mask):
    pairs = [(source, source ^ mask) for source in range(lax.axis_size(axis))]
    return lax.ppermute(value, axis, pairs)


def inner_start(width):
    return pl.multiple_of((1 - lax.axis_index("range")) * (width - HALO), HALO)


def tables_kernel(level, span, off, idx, base, slope, table, shift_ref, taps_ref, phase_ref):
    angles = off.shape[2] // 2
    half = lax.axis_index("aper") >> level & 1
    start = lax.axis_index("range") * span
    taps_count = table.shape[0]
    for order in range(2):
        role = half if order == 0 else 1 - half
        for j in range(angles // LANES):
            lane = pl.ds(pl.multiple_of(half * angles + j * LANES, LANES), LANES)

            def row(ref):
                both = ref[level, :, lane]
                return jnp.broadcast_to(jnp.where(role == 0, both[0:1], both[1:2]), (ROWS, LANES))

            shift = row(off) + (HALO - 3)
            shift_ref[order, j] = shift
            which = row(idx)
            taps = jnp.zeros((taps_count, LANES), jnp.float32)
            for k in range(table.shape[1]):
                taps = jnp.where(which == k, table[:, k : k + 1], taps)
            odd = shift & 1
            zero = jnp.zeros((ROWS, LANES), jnp.float32)
            rows = [jnp.broadcast_to(taps[t : t + 1], (ROWS, LANES)) for t in range(taps_count)]
            for t in range(taps_count + 1):
                even_tap = rows[t] if t < taps_count else zero
                odd_tap = rows[t - 1] if t > 0 else zero
                taps_ref[order, j, t] = jnp.where(odd == 1, odd_tap, even_tap)
            s = row(slope)
            ramp = lax.broadcasted_iota(jnp.int32, (ROWS, LANES), 0)
            near = row(base) + s * (ramp + start).astype(jnp.float32)
            c0, s0 = jnp.cos(near), jnp.sin(near)
            steps = span // ROWS
            far_at = lax.broadcasted_iota(jnp.int32, (steps, LANES), 0) * ROWS
            far = jnp.broadcast_to(s[0:1], (steps, LANES)) * far_at.astype(jnp.float32)
            c1, s1 = jnp.cos(far), jnp.sin(far)
            for u in range(steps):
                cu, su = c1[u : u + 1], s1[u : u + 1]
                at = pl.ds(u * ROWS, ROWS)
                phase_ref[order, 0, j, at, :] = c0 * cu - s0 * su
                phase_ref[order, 1, j, at, :] = s0 * cu + c0 * su


def turn_kernel(image, turned, edge):
    for part in range(image.shape[0]):
        turned[part] = image[part].T
    edge[...] = turned[:, pl.ds(inner_start(turned.shape[1]), HALO), :]


def shift_filter(slab, part, j, shift, taps, tmp, count):
    v = slab[part, j, 0 : count + 64, :]
    pick = lambda bit, a, b: jnp.where(
        jnp.broadcast_to((shift >> bit & 1 == 1)[None], (a.shape[0] // ROWS, ROWS, LANES)).reshape(a.shape), a, b
    )
    v = jnp.concatenate([pick(5, v[32 : count + 64], v[: count + 32]), v[count + 32 : count + 40]], 0)
    v = pick(4, v[16 : count + 40], v[: count + 24])
    v = pick(3, v[8 : count + 24], v[: count + 16])
    tmp[0, 0 : count + 16] = v
    v = pick(2, tmp[0, 4 : count + 20], v)
    tmp[1, 0 : count + 16] = v
    v = pick(1, tmp[1, 2 : count + 18], v)
    tmp[2, 0 : count + 16] = v
    total = None
    for t in range(taps.shape[0]):
        tap = jnp.broadcast_to(taps[t][None], (count // ROWS, ROWS, LANES)).reshape(count, LANES)
        term = tap * (v[:count] if t == 0 else tmp[2, t : t + count])
        total = term if total is None else total + term
    return total


def level_kernel(level, final, own, own_edge, other, other_edge, matrix, shift_ref, taps_ref, phase_ref, *rest):
    if final:
        out, slab, tmp, merged = rest
    else:
        merged, edge, slab, tmp = rest
    parts, span, angles = own.shape
    half = lax.axis_index("aper") >> level & 1
    place = lax.axis_index("range")
    rows = matrix[pl.ds(pl.multiple_of(half * angles, angles), angles), :]
    dims = (((1,), (1,)), ((), ()))
    for order, (image, image_edge) in enumerate(((own, own_edge), (other, other_edge))):
        for part in range(parts):
            inter = lax.dot_general(image[part], rows, dims, preferred_element_type=jnp.float32)
            inter = inter.astype(jnp.bfloat16).astype(jnp.float32)
            at_edge = lax.dot_general(image_edge[part], rows, dims, preferred_element_type=jnp.float32)
            at_edge = at_edge.astype(jnp.bfloat16).astype(jnp.float32)
            for j in range(angles // LANES):
                cut = slice(j * LANES, (j + 1) * LANES)
                slab[order * parts + part, j, HALO : HALO + span, :] = inter[:, cut]
                far = pl.multiple_of((1 - place) * (span + HALO), HALO)
                slab[order * parts + part, j, pl.ds(far, HALO), :] = at_edge[:, cut]
                none = pl.multiple_of(place * (span + HALO), HALO)
                slab[order * parts + part, j, pl.ds(none, HALO), :] = jnp.zeros((HALO, LANES), jnp.float32)

    def tile(j, carry):
        lane = pl.ds(pl.multiple_of(j * LANES, LANES), LANES)
        real = imag = None
        for order in range(2):
            shift = shift_ref[order, j]
            taps = taps_ref[order, j]
            re = shift_filter(slab, order * parts, j, shift, taps, tmp.at[0], span)
            im = shift_filter(slab, order * parts + 1, j, shift, taps, tmp.at[1], span)
            c, s = phase_ref[order, 0, j], phase_ref[order, 1, j]
            new_re, new_im = re * c - im * s, re * s + im * c
            real = new_re if real is None else real + new_re
            imag = new_im if imag is None else imag + new_im
        merged[0, :, lane] = real.astype(jnp.bfloat16)
        merged[1, :, lane] = imag.astype(jnp.bfloat16)
        return carry

    lax.fori_loop(0, angles // LANES, tile, 0)
    if final:
        for part in range(parts):
            out[part] = merged[part].T
    else:
        edge[...] = merged[:, pl.ds(inner_start(span), HALO), :]


def body(images, interp_matrix, offsets, tap_index, tap_table, phase_base, phase_slope):
    image = images[0]
    parts, angles, span = image.shape
    levels = offsets.shape[0]
    tiles = angles // LANES
    taps_count = tap_table.shape[1]
    f32, bf16 = jnp.float32, jnp.bfloat16
    like = jax.ShapeDtypeStruct
    turned_shape = [like((parts, span, angles), bf16), like((parts, HALO, angles), bf16)]
    work = [
        pltpu.VMEM((2 * parts, tiles, span + 2 * HALO, LANES), f32),
        pltpu.VMEM((parts, 3, span + 24, LANES), f32),
    ]

    received = from_partner(image, "aper", 1)
    current, edge = run(turn_kernel, turned_shape, [image])
    table = tap_table.T
    tables = [
        run(
            functools.partial(tables_kernel, level, span),
            [
                like((2, tiles, ROWS, LANES), jnp.int32),
                like((2, tiles, taps_count + 1, ROWS, LANES), f32),
                like((2, 2, tiles, span, LANES), f32),
            ],
            [offsets, tap_index, phase_base, phase_slope, table],
        )
        for level in range(levels)
    ]
    for level in range(levels):
        own_edge = from_partner(edge, "range", 1)
        if level == 0:
            other, other_edge = run(turn_kernel, turned_shape, [received])
        else:
            other = from_partner(current, "aper", 2**level)
            start = (1 - lax.axis_index("range")) * (span - HALO)
            other_edge = lax.dynamic_slice_in_dim(other, start, HALO, 1)
        other_edge = from_partner(other_edge, "range", 1)
        final = level == levels - 1
        outs = [like(image.shape, bf16)] if final else turned_shape
        result = run(
            functools.partial(level_kernel, level, final),
            outs,
            [current, own_edge, other, other_edge, interp_matrix, *tables[level]],
            work + ([pltpu.VMEM((parts, span, angles), bf16)] if final else []),
        )
        if final:
            return result[0][None]
        current, edge = result


def solution(mesh):
    return jax.shard_map(
        body,
        mesh=mesh,
        in_specs=(P(("scene", "aper"), None, None, "range"), P(), P(), P(), P(), P(), P()),
        out_specs=P(("scene", "aper"), None, None, "range"),
        check_vma=False,
    )
```

```python
import functools

import jax
import jax.numpy as jnp
from jax import lax
from jax.experimental import pallas as pl
from jax.experimental.pallas import tpu as pltpu
from jax.sharding import PartitionSpec as P

HALO = 32
LANES = 128
ROWS = 8
KERNEL_VMEM = 8 << 20
VMEM = pl.BlockSpec(memory_space=pltpu.VMEM)
like = jax.ShapeDtypeStruct
f32, bf16 = jnp.float32, jnp.bfloat16


def run(kernel, outs, args, scratch=(), flops=0):
    size = sum(o.size * o.dtype.itemsize for o in [*outs, *args])
    return pl.pallas_call(
        kernel,
        out_shape=outs,
        in_specs=[VMEM] * len(args),
        out_specs=[VMEM] * len(outs),
        scratch_shapes=scratch,
        compiler_params=pltpu.CompilerParams(vmem_limit_bytes=KERNEL_VMEM),
        cost_estimate=pl.CostEstimate(flops=flops, bytes_accessed=size, transcendentals=0),
    )(*args)


def from_partner(value, axis, mask):
    pairs = [(source, source ^ mask) for source in range(lax.axis_size(axis))]
    return lax.ppermute(value, axis, pairs)


def first_bin(span, near, far):
    return pl.multiple_of(jnp.where(lax.axis_index("range") == 0, near, span - far), HALO)


def own_half(level):
    return lax.axis_index("aper") >> level & 1


def turn_kernel(image, turned, edge):
    span = turned.shape[1]
    for part in range(image.shape[0]):
        turned[part] = image[part].T
    edge[...] = turned[:, pl.ds(first_bin(span, span - HALO, span), HALO), :]


def halves_kernel(matrix, halves):
    angles = matrix.shape[1]
    for half in range(halves.shape[0]):
        halves[half] = matrix[half * angles : (half + 1) * angles, :].T


def make_tables(level, span, order, params, shift_ref, taps_ref, phase_ref):
    off, idx, base, slope, table = params
    angles = off.shape[2] // 2
    half = own_half(level)
    start = lax.axis_index("range") * span
    taps_count = table.shape[0]
    role = half if order == 0 else 1 - half
    for j in range(angles // LANES):
        lane = pl.ds(pl.multiple_of(half * angles + j * LANES, LANES), LANES)

        def row(ref):
            both = ref[level, :, lane]
            return jnp.broadcast_to(jnp.where(role == 0, both[0:1], both[1:2]), (ROWS, LANES))

        shift = row(off) + (HALO - 3)
        shift_ref[j] = shift
        which = row(idx)
        taps = jnp.zeros((taps_count, LANES), f32)
        for k in range(table.shape[1]):
            taps = jnp.where(which == k, table[:, k : k + 1], taps)
        odd = shift & 1
        zero = jnp.zeros((ROWS, LANES), f32)
        rows = [jnp.broadcast_to(taps[t : t + 1], (ROWS, LANES)) for t in range(taps_count)]
        for t in range(taps_count + 1):
            even_tap = rows[t] if t < taps_count else zero
            odd_tap = rows[t - 1] if t > 0 else zero
            taps_ref[j, t] = jnp.where(odd == 1, odd_tap, even_tap)
        s = row(slope)
        ramp = lax.broadcasted_iota(jnp.int32, (ROWS, LANES), 0)
        near = row(base) + s * (ramp + start).astype(f32)
        c0, s0 = jnp.cos(near), jnp.sin(near)
        steps = span // ROWS
        far_at = lax.broadcasted_iota(jnp.int32, (steps, LANES), 0) * ROWS
        far = jnp.broadcast_to(s[0:1], (steps, LANES)) * far_at.astype(f32)
        c1, s1 = jnp.cos(far), jnp.sin(far)
        for u in range(steps):
            cu, su = c1[u : u + 1], s1[u : u + 1]
            at = pl.ds(u * ROWS, ROWS)
            phase_ref[0, j, at, :] = c0 * cu - s0 * su
            phase_ref[1, j, at, :] = s0 * cu + c0 * su


def interpolate(level, span, pieces, halves, slab):
    half = own_half(level)
    rows = jnp.concatenate([ref[part] for ref, _, _ in pieces for part in range(ref.shape[0])], 0)
    inter = jnp.dot(rows, halves[half], preferred_element_type=f32).astype(bf16).astype(f32)
    at = 0
    for ref, near, far in pieces:
        place = pl.ds(pl.multiple_of(first_bin(span, near, far) + HALO, HALO), far - near)
        for part in range(ref.shape[0]):
            for j in range(inter.shape[1] // LANES):
                slab[part, j, place, :] = inter[at : at + far - near, j * LANES : (j + 1) * LANES]
            at += far - near
    place = pl.ds(pl.multiple_of(first_bin(span, -HALO, 0) + HALO, HALO), HALO)
    slab[:, :, place, :] = jnp.zeros((slab.shape[0], slab.shape[1], HALO, LANES), f32)


def pick(shift, bit, a, b):
    count = a.shape[0]
    mask = jnp.broadcast_to((shift >> bit & 1 == 1)[None], (count // ROWS, ROWS, LANES))
    return jnp.where(mask.reshape(count, LANES), a, b)


def shift_filter(slab, part, j, start, shift, taps, tmp, count):
    v = slab[part, j, pl.ds(start, count + 64), :]
    v = jnp.concatenate([pick(shift, 5, v[32 : count + 64], v[: count + 32]), v[count + 32 : count + 40]], 0)
    v = pick(shift, 4, v[16 : count + 40], v[: count + 24])
    v = pick(shift, 3, v[8 : count + 24], v[: count + 16])
    tmp[0, 0 : count + 16] = v
    v = pick(shift, 2, tmp[0, 4 : count + 20], v)
    tmp[1, 0 : count + 16] = v
    v = pick(shift, 1, tmp[1, 2 : count + 18], v)
    tmp[2, 0 : count + 16] = v
    total = None
    for t in range(taps.shape[0]):
        tap = jnp.broadcast_to(taps[t][None], (count // ROWS, ROWS, LANES)).reshape(count, LANES)
        term = tap * (v[:count] if t == 0 else tmp[2, t : t + count])
        total = term if total is None else total + term
    return total


def terms(slab, j, start, count, tables, tmp):
    shift_ref, taps_ref, phase_ref = tables
    shift, taps = shift_ref[j], taps_ref[j]
    re = shift_filter(slab, 0, j, start, shift, taps, tmp.at[0], count)
    im = shift_filter(slab, 1, j, start, shift, taps, tmp.at[1], count)
    c = phase_ref[0, j, pl.ds(start, count), :]
    s = phase_ref[1, j, pl.ds(start, count), :]
    return re * c - im * s, re * s + im * c


def own_kernel(level, span, stretches, *refs):
    pieces = [(ref, *stretch) for ref, stretch in zip(refs, stretches)]
    refs = refs[len(stretches) :]
    halves, params, (acc, *others), (slab, tmp, *own) = refs[0], refs[1:6], refs[6:10], refs[10:]
    make_tables(level, span, 0, params, *own)
    make_tables(level, span, 1, params, *others)
    interpolate(level, span, pieces, halves, slab)

    def tile(j, carry):
        re, im = terms(slab, j, 0, span, own, tmp)
        acc[0, j], acc[1, j] = re, im
        return carry

    lax.fori_loop(0, acc.shape[1], tile, 0)


def merge_kernel(level, span, stretches, near, far, final, *refs):
    pieces = [(ref, *stretch) for ref, stretch in zip(refs, stretches)]
    refs = refs[len(stretches) :]
    halves, acc, tables, out, slab, tmp = refs[0], refs[1], refs[2:5], refs[5], refs[6], refs[7]
    merged = refs[8] if final else out
    interpolate(level, span, pieces, halves, slab)
    start, count = first_bin(span, near, far), far - near

    def tile(j, carry):
        lane = pl.ds(pl.multiple_of(j * LANES, LANES), LANES)
        re, im = terms(slab, j, start, count, tables, tmp)
        merged[0, :, lane] = (acc[0, j, pl.ds(start, count), :] + re).astype(bf16)
        merged[1, :, lane] = (acc[1, j, pl.ds(start, count), :] + im).astype(bf16)
        return carry

    lax.fori_loop(0, acc.shape[1], tile, 0)
    if final:
        for part in range(out.shape[0]):
            out[part] = merged[part].T


def body(images, interp_matrix, offsets, tap_index, tap_table, phase_base, phase_slope):
    image = images[0]
    parts, angles, span = image.shape
    levels = offsets.shape[0]
    tiles = angles // LANES
    taps_count = tap_table.shape[1]
    params = [offsets, tap_index, phase_base, phase_slope, tap_table.T]
    table_shapes = [((tiles, ROWS, LANES), jnp.int32), ((tiles, taps_count + 1, ROWS, LANES), f32), ((2, tiles, span, LANES), f32)]

    def work(count):
        return [pltpu.VMEM((parts, tiles, span + 2 * HALO, LANES), f32), pltpu.VMEM((parts, 3, count + 24, LANES), f32)]

    def turned(value):
        return run(turn_kernel, [like((parts, span, angles), bf16), like((parts, HALO, angles), bf16)], [value])

    def own(level, pieces):
        refs, stretches = zip(*pieces)
        return run(
            functools.partial(own_kernel, level, span, stretches),
            [like((parts, tiles, span, LANES), f32)] + [like(*shape) for shape in table_shapes],
            [*refs, halves, *params],
            work(span) + [pltpu.VMEM(*shape) for shape in table_shapes],
        )

    def merge(level, pieces, near, far, own_terms, final=False):
        refs, stretches = zip(*pieces)
        shape = image.shape if final else (parts, far - near, angles)
        return run(
            functools.partial(merge_kernel, level, span, stretches, near, far, final),
            [like(shape, bf16)],
            [*refs, halves, *own_terms],
            work(far - near) + ([pltpu.VMEM((parts, span, angles), bf16)] if final else []),
        )[0]

    def swap(value):
        return from_partner(value, "range", 1)

    received = from_partner(image, "aper", 1)
    (halves,) = run(halves_kernel, [like((2, angles, angles), bf16)], [interp_matrix])

    current, edge = turned(image)
    beyond = (span, span + HALO)
    own_terms = own(0, [(current, (0, span)), (swap(edge), beyond)])
    other, other_edge = turned(received)
    other_edge = swap(other_edge)
    cut = span - HALO
    outer = merge(0, [(other, (0, span))], 0, cut, own_terms)
    inner = merge(0, [(other, (0, span)), (other_edge, beyond)], cut, span, own_terms)

    other_outer = from_partner(outer, "aper", 2)
    other_inner = from_partner(inner, "aper", 2)
    own_terms = own(1, [(outer, (0, cut)), (inner, (cut, span)), (swap(inner), beyond)])
    middle = cut - HALO
    outer = merge(1, [(other_outer, (0, cut))], 0, middle, own_terms)
    inner = merge(
        1, [(other_outer, (0, cut)), (other_inner, (cut, span)), (swap(other_inner), beyond)], middle, span, own_terms
    )

    def last(value):
        start = jnp.where(lax.axis_index("range") == 0, span - middle - HALO, 0)
        return lax.dynamic_slice_in_dim(value, start, HALO, 1)

    other_outer = from_partner(outer, "aper", 4)
    other_inner = from_partner(inner, "aper", 4)
    own_terms = own(2, [(outer, (0, middle)), (inner, (middle, span)), (swap(last(inner)), beyond)])
    pieces = [(other_outer, (0, middle)), (other_inner, (middle, span)), (swap(last(other_inner)), beyond)]
    return merge(2, pieces, 0, span, own_terms, True)[None]


def solution(mesh):
    return jax.shard_map(
        body,
        mesh=mesh,
        in_specs=(P(("scene", "aper"), None, None, "range"), P(), P(), P(), P(), P(), P()),
        out_specs=P(("scene", "aper"), None, None, "range"),
        check_vma=False,
    )
```

```python
import functools

import jax
import jax.numpy as jnp
from jax import lax
from jax.experimental import pallas as pl
from jax.experimental.pallas import tpu as pltpu
from jax.sharding import PartitionSpec as P

HALO = 32
LANES = 128
ROWS = 8
STEP = 16
KERNEL_VMEM = 8 << 20
VMEM = pl.BlockSpec(memory_space=pltpu.VMEM)
like = jax.ShapeDtypeStruct
f32, bf16 = jnp.float32, jnp.bfloat16


def run(kernel, outs, args, scratch=(), flops=0):
    size = sum(o.size * o.dtype.itemsize for o in [*outs, *args])
    return pl.pallas_call(
        kernel,
        out_shape=outs,
        in_specs=[VMEM] * len(args),
        out_specs=[VMEM] * len(outs),
        scratch_shapes=scratch,
        compiler_params=pltpu.CompilerParams(vmem_limit_bytes=KERNEL_VMEM),
        cost_estimate=pl.CostEstimate(flops=flops, bytes_accessed=size, transcendentals=0),
    )(*args)


def edge_kernel(value, after, edge):
    width = value.shape[1]
    edge[...] = value[:, pl.ds(first_bin(width, width - HALO, width), HALO), :]


def inner_edge(value, after):
    return pl.pallas_call(
        edge_kernel,
        out_shape=like((value.shape[0], HALO, value.shape[2]), value.dtype),
        in_specs=[VMEM, pl.BlockSpec(memory_space=pl.ANY)],
        out_specs=VMEM,
        compiler_params=pltpu.CompilerParams(vmem_limit_bytes=KERNEL_VMEM),
        cost_estimate=pl.CostEstimate(flops=0, bytes_accessed=0, transcendentals=0),
    )(value, after)


def after_kernel(value, token, out):
    out[...] = value[...]


def after(value, token):
    return pl.pallas_call(
        after_kernel,
        out_shape=like(value.shape, value.dtype),
        in_specs=[VMEM, pl.BlockSpec(memory_space=pl.ANY)],
        out_specs=VMEM,
        compiler_params=pltpu.CompilerParams(vmem_limit_bytes=KERNEL_VMEM),
        cost_estimate=pl.CostEstimate(flops=0, bytes_accessed=0, transcendentals=0),
    )(value, token)


def from_partner(value, axis, mask):
    pairs = [(source, source ^ mask) for source in range(lax.axis_size(axis))]
    return lax.ppermute(value, axis, pairs)


def first_bin(span, near, far):
    return pl.multiple_of(jnp.where(lax.axis_index("range") == 0, near, span - far), STEP)


def own_half(level):
    return lax.axis_index("aper") >> level & 1


def turn_kernel(image, turned, edge):
    span = turned.shape[1]
    for part in range(image.shape[0]):
        turned[part] = image[part].T
    edge[...] = turned[:, pl.ds(first_bin(span, span - HALO, span), HALO), :]


def halves_kernel(matrix, halves):
    angles = matrix.shape[1]
    for half in range(halves.shape[0]):
        halves[half] = matrix[half * angles : (half + 1) * angles, :].T


def make_tables(level, span, order, params, shift_ref, taps_ref, phase_ref):
    off, idx, base, slope, table = params
    angles = off.shape[2] // 2
    half = own_half(level)
    start = lax.axis_index("range") * span
    taps_count = table.shape[0]
    role = half if order == 0 else 1 - half
    for j in range(angles // LANES):
        lane = pl.ds(pl.multiple_of(half * angles + j * LANES, LANES), LANES)

        def row(ref):
            both = ref[level, :, lane]
            return jnp.broadcast_to(jnp.where(role == 0, both[0:1], both[1:2]), (ROWS, LANES))

        shift = row(off) + (HALO - 3)
        shift_ref[j] = shift
        which = row(idx)
        taps = jnp.zeros((taps_count, LANES), f32)
        for k in range(table.shape[1]):
            taps = jnp.where(which == k, table[:, k : k + 1], taps)
        odd = shift & 1
        zero = jnp.zeros((ROWS, LANES), f32)
        rows = [jnp.broadcast_to(taps[t : t + 1], (ROWS, LANES)) for t in range(taps_count)]
        for t in range(taps_count + 1):
            even_tap = rows[t] if t < taps_count else zero
            odd_tap = rows[t - 1] if t > 0 else zero
            taps_ref[j, t] = jnp.where(odd == 1, odd_tap, even_tap)
        s = row(slope)
        ramp = lax.broadcasted_iota(jnp.int32, (ROWS, LANES), 0)
        near = row(base) + s * (ramp + start).astype(f32)
        c0, s0 = jnp.cos(near), jnp.sin(near)
        steps = span // ROWS
        far_at = lax.broadcasted_iota(jnp.int32, (steps, LANES), 0) * ROWS
        far = jnp.broadcast_to(s[0:1], (steps, LANES)) * far_at.astype(f32)
        c1, s1 = jnp.cos(far), jnp.sin(far)
        for u in range(steps):
            cu, su = c1[u : u + 1], s1[u : u + 1]
            at = pl.ds(u * ROWS, ROWS)
            phase_ref[0, j, at, :] = c0 * cu - s0 * su
            phase_ref[1, j, at, :] = s0 * cu + c0 * su


def interpolate(level, span, pieces, halves, slab):
    half = own_half(level)
    rows = jnp.concatenate([ref[part] for ref, _, _ in pieces for part in range(ref.shape[0])], 0)
    inter = jnp.dot(rows, halves[half], preferred_element_type=f32).astype(bf16).astype(f32)
    at = 0
    for ref, near, far in pieces:
        place = pl.ds(pl.multiple_of(first_bin(span, near, far) + HALO, STEP), far - near)
        for part in range(ref.shape[0]):
            for j in range(inter.shape[1] // LANES):
                slab[part, j, place, :] = inter[at : at + far - near, j * LANES : (j + 1) * LANES]
            at += far - near
    place = pl.ds(pl.multiple_of(first_bin(span, -HALO, 0) + HALO, HALO), HALO)
    slab[:, :, place, :] = jnp.zeros((slab.shape[0], slab.shape[1], HALO, LANES), f32)


def pick(shift, bit, a, b):
    count = a.shape[0]
    mask = jnp.broadcast_to((shift >> bit & 1 == 1)[None], (count // ROWS, ROWS, LANES))
    return jnp.where(mask.reshape(count, LANES), a, b)


def shift_filter(slab, part, j, start, shift, taps, tmp, count):
    v = slab[part, j, pl.ds(start, count + 64), :]
    v = jnp.concatenate([pick(shift, 5, v[32 : count + 64], v[: count + 32]), v[count + 32 : count + 40]], 0)
    v = pick(shift, 4, v[16 : count + 40], v[: count + 24])
    v = pick(shift, 3, v[8 : count + 24], v[: count + 16])
    tmp[0, 0 : count + 16] = v
    v = pick(shift, 2, tmp[0, 4 : count + 20], v)
    tmp[1, 0 : count + 16] = v
    v = pick(shift, 1, tmp[1, 2 : count + 18], v)
    tmp[2, 0 : count + 16] = v
    total = None
    for t in range(taps.shape[0]):
        tap = jnp.broadcast_to(taps[t][None], (count // ROWS, ROWS, LANES)).reshape(count, LANES)
        term = tap * (v[:count] if t == 0 else tmp[2, t : t + count])
        total = term if total is None else total + term
    return total


def terms(slab, j, start, count, tables, tmp):
    shift_ref, taps_ref, phase_ref = tables
    shift, taps = shift_ref[j], taps_ref[j]
    re = shift_filter(slab, 0, j, start, shift, taps, tmp.at[0], count)
    im = shift_filter(slab, 1, j, start, shift, taps, tmp.at[1], count)
    c = phase_ref[0, j, pl.ds(start, count), :]
    s = phase_ref[1, j, pl.ds(start, count), :]
    return re * c - im * s, re * s + im * c


def own_kernel(level, span, stretches, *refs):
    pieces = [(ref, *stretch) for ref, stretch in zip(refs, stretches)]
    refs = refs[len(stretches) :]
    halves, params, (acc, *others), (slab, tmp, *own) = refs[0], refs[1:6], refs[6:10], refs[10:]
    make_tables(level, span, 0, params, *own)
    make_tables(level, span, 1, params, *others)
    interpolate(level, span, pieces, halves, slab)

    def tile(j, carry):
        re, im = terms(slab, j, 0, span, own, tmp)
        acc[0, j], acc[1, j] = re, im
        return carry

    lax.fori_loop(0, acc.shape[1], tile, 0)


def merge_kernel(level, span, stretches, near, far, final, *refs):
    pieces = [(ref, *stretch) for ref, stretch in zip(refs, stretches)]
    refs = refs[len(stretches) :]
    halves, acc, tables = refs[0], refs[1], refs[2:5]
    start, count = first_bin(span, near, far), far - near
    if final:
        out, slab, tmp, merged = refs[-4:]
        if near > 0:
            merged[:, pl.ds(first_bin(span, 0, near), near), :] = refs[5][...]
        into = start
    else:
        merged, slab, tmp = refs[5:]
        into = 0
    interpolate(level, span, pieces, halves, slab)

    def tile(j, carry):
        lane = pl.ds(pl.multiple_of(j * LANES, LANES), LANES)
        re, im = terms(slab, j, start, count, tables, tmp)
        merged[0, pl.ds(into, count), lane] = (acc[0, j, pl.ds(start, count), :] + re).astype(bf16)
        merged[1, pl.ds(into, count), lane] = (acc[1, j, pl.ds(start, count), :] + im).astype(bf16)
        return carry

    lax.fori_loop(0, acc.shape[1], tile, 0)
    if final:
        for part in range(out.shape[0]):
            out[part] = merged[part].T


def body(images, interp_matrix, offsets, tap_index, tap_table, phase_base, phase_slope):
    image = images[0]
    parts, angles, span = image.shape
    levels = offsets.shape[0]
    tiles = angles // LANES
    taps_count = tap_table.shape[1]
    params = [offsets, tap_index, phase_base, phase_slope, tap_table.T]
    table_shapes = [((tiles, ROWS, LANES), jnp.int32), ((tiles, taps_count + 1, ROWS, LANES), f32), ((2, tiles, span, LANES), f32)]

    def work(count):
        return [pltpu.VMEM((parts, tiles, span + 2 * HALO, LANES), f32), pltpu.VMEM((parts, 3, count + 24, LANES), f32)]

    def turned(value):
        return run(turn_kernel, [like((parts, span, angles), bf16), like((parts, HALO, angles), bf16)], [value])

    def own(level, pieces):
        refs, stretches = zip(*pieces)
        return run(
            functools.partial(own_kernel, level, span, stretches),
            [like((parts, tiles, span, LANES), f32)] + [like(*shape) for shape in table_shapes],
            [*refs, halves, *params],
            work(span) + [pltpu.VMEM(*shape) for shape in table_shapes],
        )

    def merge(level, pieces, near, far, own_terms, ready=None, final=False):
        refs, stretches = zip(*pieces)
        shape = image.shape if final else (parts, far - near, angles)
        return run(
            functools.partial(merge_kernel, level, span, stretches, near, far, final),
            [like(shape, bf16)],
            [*refs, halves, *own_terms] + ([ready] if ready is not None else []),
            work(far - near) + ([pltpu.VMEM((parts, span, angles), bf16)] if final else []),
        )[0]

    def swap(value):
        return from_partner(value, "range", 1)

    received = from_partner(image, "aper", 1)
    (halves,) = run(halves_kernel, [like((2, angles, angles), bf16)], [interp_matrix])

    current, edge = turned(image)
    beyond = (span, span + HALO)
    own_terms = own(0, [(current, (0, span)), (swap(edge), beyond)])
    other, other_edge = turned(received)
    other_edge = swap(other_edge)
    cut = 96
    outer = merge(0, [(other, (0, span))], 0, cut, own_terms)
    pieces = [(other, (0, span)), (other_edge, beyond)]
    inner = merge(0, pieces, cut, span, own_terms)

    other_outer = from_partner(outer, "aper", 2)
    other_inner = from_partner(inner, "aper", 2)
    own_edge = swap(inner_edge(inner, outer))
    own_terms = own(1, [(outer, (0, cut)), (inner, (cut, span)), (own_edge, beyond)])
    middle = 64
    last = span - HALO
    outer = merge(1, [(other_outer, (0, cut))], 0, middle, own_terms)
    other_edge = swap(inner_edge(other_inner, outer))
    pieces = [(other_outer, (0, cut)), (other_inner, (cut, span)), (other_edge, beyond)]
    edge = merge(1, pieces, last, span, own_terms)
    inner = merge(1, pieces, middle, last, own_terms)

    other_outer = from_partner(outer, "aper", 4)
    other_edge = from_partner(edge, "aper", 4)
    other_inner = from_partner(inner, "aper", 4)
    own_edge = swap(edge)
    own_terms = own(2, [(outer, (0, middle)), (inner, (middle, last)), (edge, (last, span)), (own_edge, beyond)])
    pieces = [(other_outer, (0, middle)), (other_inner, (middle, last)), (other_edge, (last, span))]
    pieces += [(swap(after(other_edge, own_terms[0])), beyond)]
    first = middle - HALO
    if first > 0:
        outer = merge(2, [(other_outer, (0, middle))], 0, first, own_terms)
    else:
        outer = None
    return merge(2, pieces, first, span, own_terms, outer, True)[None]


def solution(mesh):
    return jax.shard_map(
        body,
        mesh=mesh,
        in_specs=(P(("scene", "aper"), None, None, "range"), P(), P(), P(), P(), P(), P()),
        out_specs=P(("scene", "aper"), None, None, "range"),
        check_vma=False,
    )
```

```python
import functools

import jax
import jax.numpy as jnp
from jax import lax
from jax.experimental import pallas as pl
from jax.experimental.pallas import tpu as pltpu
from jax.sharding import PartitionSpec as P

HALO = 32
LANES = 128
ROWS = 8
STEP = 16
KERNEL_VMEM = 8 << 20
VMEM = pl.BlockSpec(memory_space=pltpu.VMEM)
like = jax.ShapeDtypeStruct
f32, bf16 = jnp.float32, jnp.bfloat16


def run(kernel, outs, args, scratch=(), flops=0):
    return pl.pallas_call(
        kernel,
        out_shape=outs,
        in_specs=[VMEM] * len(args),
        out_specs=[VMEM] * len(outs),
        scratch_shapes=scratch,
        compiler_params=pltpu.CompilerParams(vmem_limit_bytes=KERNEL_VMEM),
        cost_estimate=pl.CostEstimate(flops=flops, bytes_accessed=flops // 300, transcendentals=0),
    )(*args)


def edge_kernel(value, after, edge):
    width = value.shape[1]
    edge[...] = value[:, pl.ds(first_bin(width, width - HALO, width), HALO), :]


def inner_edge(value, after):
    return pl.pallas_call(
        edge_kernel,
        out_shape=like((value.shape[0], HALO, value.shape[2]), value.dtype),
        in_specs=[VMEM, pl.BlockSpec(memory_space=pl.ANY)],
        out_specs=VMEM,
        compiler_params=pltpu.CompilerParams(vmem_limit_bytes=KERNEL_VMEM),
        cost_estimate=pl.CostEstimate(flops=0, bytes_accessed=0, transcendentals=0),
    )(value, after)


def after_kernel(value, token, out):
    out[...] = value[...]


def after(value, token):
    return pl.pallas_call(
        after_kernel,
        out_shape=like(value.shape, value.dtype),
        in_specs=[VMEM, pl.BlockSpec(memory_space=pl.ANY)],
        out_specs=VMEM,
        compiler_params=pltpu.CompilerParams(vmem_limit_bytes=KERNEL_VMEM),
        cost_estimate=pl.CostEstimate(flops=0, bytes_accessed=0, transcendentals=0),
    )(value, token)


def from_partner(value, axis, mask):
    pairs = [(source, source ^ mask) for source in range(lax.axis_size(axis))]
    return lax.ppermute(value, axis, pairs)


def first_bin(span, near, far):
    return pl.multiple_of(jnp.where(lax.axis_index("range") == 0, near, span - far), STEP)


def own_half(level):
    return lax.axis_index("aper") >> level & 1


def turn_kernel(image, turned, edge):
    span = turned.shape[1]
    for part in range(image.shape[0]):
        turned[part] = image[part].T
    edge[...] = turned[:, pl.ds(first_bin(span, span - HALO, span), HALO), :]


def halves_kernel(matrix, halves):
    angles = matrix.shape[1]
    for half in range(halves.shape[0]):
        halves[half] = matrix[half * angles : (half + 1) * angles, :].T


def make_tables(level, span, order, params, shift_ref, taps_ref, phase_ref):
    off, idx, base, slope, table = params
    angles = off.shape[2] // 2
    half = own_half(level)
    start = lax.axis_index("range") * span
    taps_count = table.shape[0]
    role = half if order == 0 else 1 - half
    for j in range(angles // LANES):
        lane = pl.ds(pl.multiple_of(half * angles + j * LANES, LANES), LANES)

        def row(ref):
            both = ref[level, :, lane]
            return jnp.broadcast_to(jnp.where(role == 0, both[0:1], both[1:2]), (ROWS, LANES))

        shift = row(off) + (HALO - 3)
        shift_ref[j] = shift
        which = row(idx)
        taps = jnp.zeros((taps_count, LANES), f32)
        for k in range(table.shape[1]):
            taps = jnp.where(which == k, table[:, k : k + 1], taps)
        odd = shift & 1
        zero = jnp.zeros((ROWS, LANES), f32)
        rows = [jnp.broadcast_to(taps[t : t + 1], (ROWS, LANES)) for t in range(taps_count)]
        for t in range(taps_count + 1):
            even_tap = rows[t] if t < taps_count else zero
            odd_tap = rows[t - 1] if t > 0 else zero
            taps_ref[j, t] = jnp.where(odd == 1, odd_tap, even_tap)
        s = row(slope)
        ramp = lax.broadcasted_iota(jnp.int32, (ROWS, LANES), 0)
        near = row(base) + s * (ramp + start).astype(f32)
        c0, s0 = jnp.cos(near), jnp.sin(near)
        steps = span // ROWS
        far_at = lax.broadcasted_iota(jnp.int32, (steps, LANES), 0) * ROWS
        far = jnp.broadcast_to(s[0:1], (steps, LANES)) * far_at.astype(f32)
        c1, s1 = jnp.cos(far), jnp.sin(far)
        for u in range(steps):
            cu, su = c1[u : u + 1], s1[u : u + 1]
            at = pl.ds(u * ROWS, ROWS)
            phase_ref[0, j, at, :] = c0 * cu - s0 * su
            phase_ref[1, j, at, :] = s0 * cu + c0 * su


def interpolate(level, span, pieces, halves, slab):
    half = own_half(level)
    rows = jnp.concatenate([ref[part] for ref, _, _ in pieces for part in range(ref.shape[0])], 0)
    inter = jnp.dot(rows, halves[half], preferred_element_type=f32).astype(bf16).astype(f32)
    at = 0
    for ref, near, far in pieces:
        place = pl.ds(pl.multiple_of(first_bin(span, near, far) + HALO, STEP), far - near)
        for part in range(ref.shape[0]):
            for j in range(inter.shape[1] // LANES):
                slab[part, j, place, :] = inter[at : at + far - near, j * LANES : (j + 1) * LANES]
            at += far - near
    place = pl.ds(pl.multiple_of(first_bin(span, -HALO, 0) + HALO, HALO), HALO)
    slab[:, :, place, :] = jnp.zeros((slab.shape[0], slab.shape[1], HALO, LANES), f32)


def pick(shift, bit, a, b):
    count = a.shape[0]
    mask = jnp.broadcast_to((shift >> bit & 1 == 1)[None], (count // ROWS, ROWS, LANES))
    return jnp.where(mask.reshape(count, LANES), a, b)


def shift_filter(slab, part, j, start, shift, taps, tmp, count):
    v = slab[part, j, pl.ds(start, count + 64), :]
    v = jnp.concatenate([pick(shift, 5, v[32 : count + 64], v[: count + 32]), v[count + 32 : count + 40]], 0)
    v = pick(shift, 4, v[16 : count + 40], v[: count + 24])
    v = pick(shift, 3, v[8 : count + 24], v[: count + 16])
    tmp[0, 0 : count + 16] = v
    v = pick(shift, 2, tmp[0, 4 : count + 20], v)
    tmp[1, 0 : count + 16] = v
    v = pick(shift, 1, tmp[1, 2 : count + 18], v)
    tmp[2, 0 : count + 16] = v
    total = None
    for t in range(taps.shape[0]):
        tap = jnp.broadcast_to(taps[t][None], (count // ROWS, ROWS, LANES)).reshape(count, LANES)
        term = tap * (v[:count] if t == 0 else tmp[2, t : t + count])
        total = term if total is None else total + term
    return total


def terms(slab, j, start, count, tables, tmp):
    shift_ref, taps_ref, phase_ref = tables
    shift, taps = shift_ref[j], taps_ref[j]
    re = shift_filter(slab, 0, j, start, shift, taps, tmp.at[0], count)
    im = shift_filter(slab, 1, j, start, shift, taps, tmp.at[1], count)
    c = phase_ref[0, j, pl.ds(start, count), :]
    s = phase_ref[1, j, pl.ds(start, count), :]
    return re * c - im * s, re * s + im * c


def own_kernel(level, span, stretches, *refs):
    pieces = [(ref, *stretch) for ref, stretch in zip(refs, stretches)]
    refs = refs[len(stretches) :]
    halves, params, (acc, *others), (slab, tmp, *own) = refs[0], refs[1:6], refs[6:10], refs[10:]
    make_tables(level, span, 0, params, *own)
    make_tables(level, span, 1, params, *others)
    interpolate(level, span, pieces, halves, slab)

    def tile(j, carry):
        re, im = terms(slab, j, 0, span, own, tmp)
        acc[0, j], acc[1, j] = re, im
        return carry

    lax.fori_loop(0, acc.shape[1], tile, 0)


def merge_kernel(level, span, stretches, near, far, final, *refs):
    pieces = [(ref, *stretch) for ref, stretch in zip(refs, stretches)]
    refs = refs[len(stretches) :]
    halves, acc, tables = refs[0], refs[1], refs[2:5]
    start, count = first_bin(span, near, far), far - near
    if final:
        out, slab, tmp, merged = refs[-4:]
        if near > 0:
            merged[:, pl.ds(first_bin(span, 0, near), near), :] = refs[5][...]
        into = start
    else:
        merged, slab, tmp = refs[5:]
        into = 0
    interpolate(level, span, pieces, halves, slab)

    def tile(j, carry):
        lane = pl.ds(pl.multiple_of(j * LANES, LANES), LANES)
        re, im = terms(slab, j, start, count, tables, tmp)
        merged[0, pl.ds(into, count), lane] = (acc[0, j, pl.ds(start, count), :] + re).astype(bf16)
        merged[1, pl.ds(into, count), lane] = (acc[1, j, pl.ds(start, count), :] + im).astype(bf16)
        return carry

    lax.fori_loop(0, acc.shape[1], tile, 0)
    if final:
        for part in range(out.shape[0]):
            out[part] = merged[part].T


def body(images, interp_matrix, offsets, tap_index, tap_table, phase_base, phase_slope):
    image = images[0]
    parts, angles, span = image.shape
    levels = offsets.shape[0]
    tiles = angles // LANES
    taps_count = tap_table.shape[1]
    params = [offsets, tap_index, phase_base, phase_slope, tap_table.T]
    table_shapes = [((tiles, ROWS, LANES), jnp.int32), ((tiles, taps_count + 1, ROWS, LANES), f32), ((2, tiles, span, LANES), f32)]

    def work(count):
        return [pltpu.VMEM((parts, tiles, span + 2 * HALO, LANES), f32), pltpu.VMEM((parts, 3, count + 24, LANES), f32)]

    def turned(value):
        return run(turn_kernel, [like((parts, span, angles), bf16), like((parts, HALO, angles), bf16)], [value])

    def own(level, pieces):
        refs, stretches = zip(*pieces)
        return run(
            functools.partial(own_kernel, level, span, stretches),
            [like((parts, tiles, span, LANES), f32)] + [like(*shape) for shape in table_shapes],
            [*refs, halves, *params],
            work(span) + [pltpu.VMEM(*shape) for shape in table_shapes],
        )

    def merge(level, pieces, near, far, own_terms, ready=None, final=False, flops=0):
        refs, stretches = zip(*pieces)
        shape = image.shape if final else (parts, far - near, angles)
        return run(
            functools.partial(merge_kernel, level, span, stretches, near, far, final),
            [like(shape, bf16)],
            [*refs, halves, *own_terms] + ([ready] if ready is not None else []),
            work(far - near) + ([pltpu.VMEM((parts, span, angles), bf16)] if final else []),
            flops=flops,
        )[0]

    def swap(value):
        return from_partner(value, "range", 1)

    received = from_partner(image, "aper", 1)
    (halves,) = run(halves_kernel, [like((2, angles, angles), bf16)], [interp_matrix])

    current, edge = turned(image)
    beyond = (span, span + HALO)
    own_terms = own(0, [(current, (0, span)), (swap(edge), beyond)])
    other, other_edge = turned(received)
    other_edge = swap(other_edge)
    cut = 96
    outer = merge(0, [(other, (0, span))], 0, cut, own_terms, flops=0)
    pieces = [(other, (0, span)), (other_edge, beyond)]
    inner = merge(0, pieces, cut, span, own_terms, flops=0)

    other_outer = from_partner(outer, "aper", 2)
    other_inner = from_partner(inner, "aper", 2)
    own_edge = swap(inner)
    other_edge = from_partner(own_edge, "aper", 2)
    own_terms = own(1, [(outer, (0, cut)), (inner, (cut, span)), (own_edge, beyond)])
    middle = 64
    last = span - HALO
    outer = merge(1, [(other_outer, (0, cut))], 0, middle, own_terms, flops=0)
    pieces = [(other_outer, (0, cut)), (other_inner, (cut, span)), (other_edge, beyond)]
    edge = merge(1, pieces, last, span, own_terms, flops=0)
    inner = merge(1, pieces, middle, last, own_terms, flops=0)

    other_outer = from_partner(outer, "aper", 4)
    other_edge = from_partner(edge, "aper", 4)
    other_inner = from_partner(inner, "aper", 4)
    own_edge = swap(edge)
    own_terms = own(2, [(outer, (0, middle)), (inner, (middle, last)), (edge, (last, span)), (own_edge, beyond)])
    pieces = [(other_outer, (0, middle)), (other_inner, (middle, last)), (other_edge, (last, span))]
    pieces += [(swap(after(other_edge, own_terms[0])), beyond)]
    first = middle - HALO
    if first > 0:
        outer = merge(2, [(other_outer, (0, middle))], 0, first, own_terms)
    else:
        outer = None
    return merge(2, pieces, first, span, own_terms, outer, True)[None]


def solution(mesh):
    return jax.shard_map(
        body,
        mesh=mesh,
        in_specs=(P(("scene", "aper"), None, None, "range"), P(), P(), P(), P(), P(), P()),
        out_specs=P(("scene", "aper"), None, None, "range"),
        check_vma=False,
    )
```

```python
import functools

import jax
import jax.numpy as jnp
from jax import lax
from jax.experimental import pallas as pl
from jax.experimental.pallas import tpu as pltpu
from jax.sharding import PartitionSpec as P

HALO = 32
LANES = 128
ROWS = 8
STEP = 16
KERNEL_VMEM = 8 << 20
AFTER = {"m0i": "own1a", "own1b": "m1o", "copy2": "own2"}
WORK = {"m1i": 3000000000}
VMEM = pl.BlockSpec(memory_space=pltpu.VMEM)
like = jax.ShapeDtypeStruct
f32, bf16 = jnp.float32, jnp.bfloat16


def run(name, kernel, outs, args, scratch=(), token=None, flops=0):
    tokens = [] if token is None else [token]

    def without_token(*refs):
        kernel(*refs[: len(args)], *refs[len(args) + len(tokens) :])

    return pl.pallas_call(
        without_token,
        out_shape=outs,
        in_specs=[VMEM] * len(args) + [pl.BlockSpec(memory_space=pl.ANY)] * len(tokens),
        out_specs=[VMEM] * len(outs),
        scratch_shapes=scratch,
        name=name,
        compiler_params=pltpu.CompilerParams(vmem_limit_bytes=KERNEL_VMEM),
        cost_estimate=pl.CostEstimate(flops=flops, bytes_accessed=0, transcendentals=0),
    )(*args, *tokens)


def from_partner(value, axis, mask):
    pairs = [(source, source ^ mask) for source in range(lax.axis_size(axis))]
    return lax.ppermute(value, axis, pairs)


def first_bin(span, near, far):
    return pl.multiple_of(jnp.where(lax.axis_index("range") == 0, near, span - far), STEP)


def own_half(level):
    return lax.axis_index("aper") >> level & 1


def turn(image, turned, edge):
    span = turned.shape[1]
    for part in range(image.shape[0]):
        turned[part] = image[part].T
    edge[...] = turned[:, pl.ds(first_bin(span, span - HALO, span), HALO), :]


def halves_kernel(matrix, halves):
    angles = matrix.shape[1]
    for half in range(halves.shape[0]):
        halves[half] = matrix[half * angles : (half + 1) * angles, :].T


def edge_kernel(value, edge):
    width = value.shape[1]
    edge[...] = value[:, pl.ds(first_bin(width, width - HALO, width), HALO), :]


def copy_kernel(source, target):
    target[...] = source[...]


def tables_kernel(span, first_level, off, idx, base, slope, table, shift_ref, taps_ref, phase_ref):
    angles = off.shape[2] // 2
    start = lax.axis_index("range") * span
    taps_count = table.shape[0]
    columns = [jnp.broadcast_to(table[:, k : k + 1], (taps_count, LANES)) for k in range(table.shape[1])]

    def tile(at, carry):
        here, j = at // (angles // LANES), lax.rem(at, angles // LANES)
        level = here + first_level
        half = lax.axis_index("aper") >> level & 1
        lane = pl.ds(pl.multiple_of(half * angles + j * LANES, LANES), LANES)
        for order in range(2):
            role = half if order == 0 else 1 - half

            def row(ref):
                both = ref[level, :, lane]
                return jnp.broadcast_to(jnp.where(role == 0, both[0:1], both[1:2]), (ROWS, LANES))

            shift = row(off) + (HALO - 3)
            shift_ref[here, order, j] = shift
            which = row(idx)
            taps = jnp.zeros((taps_count, LANES), f32)
            for k, column in enumerate(columns):
                taps = jnp.where(which == k, column, taps)
            odd = shift & 1
            zero = jnp.zeros((ROWS, LANES), f32)
            rows = [jnp.broadcast_to(taps[t : t + 1], (ROWS, LANES)) for t in range(taps_count)]
            for t in range(taps_count + 1):
                even_tap = rows[t] if t < taps_count else zero
                odd_tap = rows[t - 1] if t > 0 else zero
                taps_ref[here, order, j, t] = jnp.where(odd == 1, odd_tap, even_tap)
            s = row(slope)
            ramp = lax.broadcasted_iota(jnp.int32, (ROWS, LANES), 0)
            near = row(base) + s * (ramp + start).astype(f32)
            c0, s0 = jnp.cos(near), jnp.sin(near)
            steps = span // ROWS
            far_at = lax.broadcasted_iota(jnp.int32, (steps, LANES), 0) * ROWS
            far = jnp.broadcast_to(s[0:1], (steps, LANES)) * far_at.astype(f32)
            c1, s1 = jnp.cos(far), jnp.sin(far)
            for u in range(steps):
                cu, su = c1[u : u + 1], s1[u : u + 1]
                bins = pl.ds(u * ROWS, ROWS)
                phase_ref[here, order, 0, j, bins, :] = c0 * cu - s0 * su
                phase_ref[here, order, 1, j, bins, :] = s0 * cu + c0 * su
        return carry

    lax.fori_loop(0, shift_ref.shape[0] * (angles // LANES), tile, 0)


def interpolate(level, span, pieces, halves, slab):
    rows = jnp.concatenate([ref[part] for ref, _, _ in pieces for part in range(ref.shape[0])], 0)
    inter = jnp.dot(rows, halves[own_half(level)], preferred_element_type=f32).astype(bf16).astype(f32)
    at = 0
    for ref, near, far in pieces:
        place = pl.ds(pl.multiple_of(first_bin(span, near, far) + HALO, STEP), far - near)
        for part in range(ref.shape[0]):
            for j in range(inter.shape[1] // LANES):
                slab[part, j, place, :] = inter[at : at + far - near, j * LANES : (j + 1) * LANES]
            at += far - near
    place = pl.ds(pl.multiple_of(first_bin(span, -HALO, 0) + HALO, HALO), HALO)
    slab[:, :, place, :] = jnp.zeros((slab.shape[0], slab.shape[1], HALO, LANES), f32)


def pick(shift, bit, a, b):
    count = a.shape[0]
    mask = jnp.broadcast_to((shift >> bit & 1 == 1)[None], (count // ROWS, ROWS, LANES))
    return jnp.where(mask.reshape(count, LANES), a, b)


def shift_filter(slab, part, j, start, shift, taps, tmp, count):
    v = slab[part, j, pl.ds(start, count + 64), :]
    v = jnp.concatenate([pick(shift, 5, v[32 : count + 64], v[: count + 32]), v[count + 32 : count + 40]], 0)
    v = pick(shift, 4, v[16 : count + 40], v[: count + 24])
    v = pick(shift, 3, v[8 : count + 24], v[: count + 16])
    tmp[0, 0 : count + 16] = v
    v = pick(shift, 2, tmp[0, 4 : count + 20], v)
    tmp[1, 0 : count + 16] = v
    v = pick(shift, 1, tmp[1, 2 : count + 18], v)
    tmp[2, 0 : count + 16] = v
    total = None
    for t in range(taps.shape[0]):
        tap = jnp.broadcast_to(taps[t][None], (count // ROWS, ROWS, LANES)).reshape(count, LANES)
        term = tap * (v[:count] if t == 0 else tmp[2, t : t + count])
        total = term if total is None else total + term
    return total


def terms(slab, j, start, count, at, order, tables, tmp):
    shift_ref, taps_ref, phase_ref = tables
    shift, taps = shift_ref[at, order, j], taps_ref[at, order, j]
    re = shift_filter(slab, 0, j, start, shift, taps, tmp.at[0], count)
    im = shift_filter(slab, 1, j, start, shift, taps, tmp.at[1], count)
    c = phase_ref[at, order, 0, j, pl.ds(start, count), :]
    s = phase_ref[at, order, 1, j, pl.ds(start, count), :]
    return re * c - im * s, re * s + im * c


def own_kernel(level, at, span, stretches, near, far, *refs):
    pieces = [(ref, *stretch) for ref, stretch in zip(refs, stretches)]
    halves, *tables, acc, slab, tmp = refs[len(stretches) :]
    interpolate(level, span, pieces, halves, slab)
    start = first_bin(span, near, far)

    def tile(j, carry):
        acc[0, j], acc[1, j] = terms(slab, j, start, far - near, at, 0, tables, tmp)
        return carry

    lax.fori_loop(0, acc.shape[1], tile, 0)


def merge_kernel(level, at, span, stretches, near, far, held, final, *refs):
    pieces = [(ref, *stretch) for ref, stretch in zip(refs, stretches)]
    halves, acc, *tables = refs[len(stretches) : len(stretches) + 5]
    refs = refs[len(stretches) + 5 :]
    start, count = first_bin(span, near, far), far - near
    if final:
        ready, out, slab, tmp, merged = refs
        merged[:, pl.ds(first_bin(span, 0, near), near), :] = ready[...]
        into = start
    else:
        merged, slab, tmp = refs
        into = 0
    interpolate(level, span, pieces, halves, slab)
    acc_rows = pl.ds(pl.multiple_of(start - first_bin(span, *held), STEP), count)

    def tile(j, carry):
        lane = pl.ds(pl.multiple_of(j * LANES, LANES), LANES)
        for part, term in enumerate(terms(slab, j, start, count, at, 1, tables, tmp)):
            merged[part, pl.ds(into, count), lane] = (acc[part, j, acc_rows, :] + term).astype(bf16)
        return carry

    lax.fori_loop(0, acc.shape[1], tile, 0)
    if final:
        for part in range(out.shape[0]):
            out[part] = merged[part].T


def body(images, interp_matrix, offsets, tap_index, tap_table, phase_base, phase_slope):
    parts, angles, span = images.shape[1:]
    levels, roles, parent = offsets.shape
    tiles = angles // LANES
    taps_count = tap_table.shape[1]
    beyond = (span, span + HALO)
    edge_out = like((parts, HALO, angles), bf16)
    turned_outs = [like((parts, span, angles), bf16), edge_out]

    def work(count):
        return [pltpu.VMEM((parts, tiles, span + 2 * HALO, LANES), f32), pltpu.VMEM((parts, 3, count + 24, LANES), f32)]

    done = {}

    def step(name, *args):
        outs = run(name, *args, token=done.get(AFTER.get(name)), flops=WORK.get(name, 0))
        done[name] = outs[0]
        return outs

    def make_tables(name, first_level, count):
        outs = [
            like((count, roles, tiles, ROWS, LANES), jnp.int32),
            like((count, roles, tiles, taps_count + 1, ROWS, LANES), f32),
            like((count, roles, 2, tiles, span, LANES), f32),
        ]
        params = [offsets, tap_index, phase_base, phase_slope, tap_table.T]
        return step(name, functools.partial(tables_kernel, span, first_level), outs, params)

    def own(name, level, pieces, near=0, far=span):
        refs, stretches = zip(*pieces)
        at, tables = (0, first_tables) if level == 0 else (level - 1, later_tables)
        kernel = functools.partial(own_kernel, level, at, span, stretches, near, far)
        return step(name, kernel, [like((parts, tiles, far - near, LANES), f32)], [*refs, halves, *tables], work(far - near))[0]

    def merge(name, level, pieces, near, far, acc, held=(0, span), ready=None):
        refs, stretches = zip(*pieces)
        at, tables = (0, first_tables) if level == 0 else (level - 1, later_tables)
        final = ready is not None
        return step(
            name,
            functools.partial(merge_kernel, level, at, span, stretches, near, far, held, final),
            [like(images.shape[1:] if final else (parts, far - near, angles), bf16)],
            [*refs, halves, acc, *tables] + ([ready] if final else []),
            work(far - near) + ([pltpu.VMEM((parts, span, angles), bf16)] if final else []),
        )[0]

    def swap(value):
        return from_partner(value, "range", 1)

    received = from_partner(images[0], "aper", 1)
    current, edge = step("turn0", turn, turned_outs, [images[0]])
    own_edge = swap(edge)
    (halves,) = step("halves", halves_kernel, [like((2, angles, angles), bf16)], [interp_matrix])
    first_tables = make_tables("tables0", 0, 1)
    acc = own("own0", 0, [(current, (0, span)), (own_edge, beyond)])
    other, other_edge = step("turn1", turn, turned_outs, [received])
    other_edge = swap(other_edge)
    cut, middle, last = 96, 64, span - HALO
    outer = merge("m0o", 0, [(other, (0, span))], 0, cut, acc)

    other_outer = from_partner(outer, "aper", 2)
    later_tables = make_tables("tables12", 1, levels - 1)
    outer_acc = own("own1a", 1, [(outer, (0, cut))], 0, middle)
    inner = merge("m0i", 0, [(other, (0, span)), (other_edge, beyond)], cut, span, acc)
    other_inner = from_partner(inner, "aper", 2)
    own_edge = swap(step("edge1", edge_kernel, [edge_out], [inner])[0])
    other_edge = from_partner(own_edge, "aper", 2)
    new_outer = merge("m1o", 1, [(other_outer, (0, cut))], 0, middle, outer_acc, (0, middle))
    acc = own("own1b", 1, [(outer, (0, cut)), (inner, (cut, span)), (own_edge, beyond)], middle, span)
    pieces = [(other_outer, (0, cut)), (other_inner, (cut, span)), (other_edge, beyond)]
    edge = merge("m1e", 1, pieces, last, span, acc, (middle, span))
    inner = merge("m1i", 1, pieces, middle, last, acc, (middle, span))
    outer = new_outer

    other_outer = from_partner(outer, "aper", 4)
    other_edge = from_partner(edge, "aper", 4)
    other_inner = from_partner(inner, "aper", 4)
    acc = own("own2", 2, [(outer, (0, middle)), (inner, (middle, last)), (edge, (last, span)), (swap(edge), beyond)])
    pieces = [(other_outer, (0, middle)), (other_inner, (middle, last)), (other_edge, (last, span))]
    pieces += [(swap(step("copy2", copy_kernel, [edge_out], [other_edge])[0]), beyond)]
    first = middle - HALO
    ready = merge("f1", 2, [(other_outer, (0, middle))], 0, first, acc)
    return merge("f2", 2, pieces, first, span, acc, ready=ready)[None]


def solution(mesh):
    return jax.shard_map(
        body,
        mesh=mesh,
        in_specs=(P(("scene", "aper"), None, None, "range"), P(), P(), P(), P(), P(), P()),
        out_specs=P(("scene", "aper"), None, None, "range"),
        check_vma=False,
    )
```

```python
import functools

import jax
import jax.numpy as jnp
from jax import lax
from jax.experimental import pallas as pl
from jax.experimental.pallas import tpu as pltpu
from jax.sharding import PartitionSpec as P

HALO = 32
LANES = 128
ROWS = 8
STEP = 16
KERNEL_VMEM = 8 << 20
AFTER = {"m0i": "m0o", "own1b": "m1o", "copy2": "own2", "copy1": "m1o", "edge1": "m0i"}
WORK = {"m1i": 3000000000, "m0o": 0, "m1o": 3000000000, "own1b": 3000000000}
VMEM = pl.BlockSpec(memory_space=pltpu.VMEM)
like = jax.ShapeDtypeStruct
f32, bf16 = jnp.float32, jnp.bfloat16


def run(name, kernel, outs, args, scratch=(), token=None, flops=0):
    tokens = [] if token is None else [token]

    def without_token(*refs):
        kernel(*refs[: len(args)], *refs[len(args) + len(tokens) :])

    return pl.pallas_call(
        without_token,
        out_shape=outs,
        in_specs=[VMEM] * len(args) + [pl.BlockSpec(memory_space=pl.ANY)] * len(tokens),
        out_specs=[VMEM] * len(outs),
        scratch_shapes=scratch,
        name=name,
        compiler_params=pltpu.CompilerParams(vmem_limit_bytes=KERNEL_VMEM),
        cost_estimate=pl.CostEstimate(flops=flops, bytes_accessed=0, transcendentals=0),
    )(*args, *tokens)


def from_partner(value, axis, mask):
    pairs = [(source, source ^ mask) for source in range(lax.axis_size(axis))]
    return lax.ppermute(value, axis, pairs)


def first_bin(span, near, far):
    return pl.multiple_of(jnp.where(lax.axis_index("range") == 0, near, span - far), STEP)


def own_half(level):
    return lax.axis_index("aper") >> level & 1


def turn(image, turned, edge):
    span = turned.shape[1]
    for part in range(image.shape[0]):
        turned[part] = image[part].T
    edge[...] = turned[:, pl.ds(first_bin(span, span - HALO, span), HALO), :]


def halves_kernel(matrix, halves):
    angles = matrix.shape[1]
    for half in range(halves.shape[0]):
        halves[half] = matrix[half * angles : (half + 1) * angles, :].T


def edge_kernel(value, edge):
    width = value.shape[1]
    edge[...] = value[:, pl.ds(first_bin(width, width - HALO, width), HALO), :]


def copy_kernel(source, target):
    target[...] = source[...]


def tables_kernel(span, first_level, off, idx, base, slope, table, shift_ref, taps_ref, phase_ref):
    angles = off.shape[2] // 2
    start = lax.axis_index("range") * span
    taps_count = table.shape[0]
    columns = [jnp.broadcast_to(table[:, k : k + 1], (taps_count, LANES)) for k in range(table.shape[1])]

    def tile(at, carry):
        here, j = at // (angles // LANES), lax.rem(at, angles // LANES)
        level = here + first_level
        half = lax.axis_index("aper") >> level & 1
        lane = pl.ds(pl.multiple_of(half * angles + j * LANES, LANES), LANES)
        for order in range(2):
            role = half if order == 0 else 1 - half

            def row(ref):
                both = ref[level, :, lane]
                return jnp.broadcast_to(jnp.where(role == 0, both[0:1], both[1:2]), (ROWS, LANES))

            shift = row(off) + (HALO - 3)
            shift_ref[here, order, j] = shift
            which = row(idx)
            taps = jnp.zeros((taps_count, LANES), f32)
            for k, column in enumerate(columns):
                taps = jnp.where(which == k, column, taps)
            odd = shift & 1
            zero = jnp.zeros((ROWS, LANES), f32)
            rows = [jnp.broadcast_to(taps[t : t + 1], (ROWS, LANES)) for t in range(taps_count)]
            for t in range(taps_count + 1):
                even_tap = rows[t] if t < taps_count else zero
                odd_tap = rows[t - 1] if t > 0 else zero
                taps_ref[here, order, j, t] = jnp.where(odd == 1, odd_tap, even_tap)
            s = row(slope)
            ramp = lax.broadcasted_iota(jnp.int32, (ROWS, LANES), 0)
            near = row(base) + s * (ramp + start).astype(f32)
            c0, s0 = jnp.cos(near), jnp.sin(near)
            steps = span // ROWS
            far_at = lax.broadcasted_iota(jnp.int32, (steps, LANES), 0) * ROWS
            far = jnp.broadcast_to(s[0:1], (steps, LANES)) * far_at.astype(f32)
            c1, s1 = jnp.cos(far), jnp.sin(far)
            for u in range(steps):
                cu, su = c1[u : u + 1], s1[u : u + 1]
                bins = pl.ds(u * ROWS, ROWS)
                phase_ref[here, order, 0, j, bins, :] = c0 * cu - s0 * su
                phase_ref[here, order, 1, j, bins, :] = s0 * cu + c0 * su
        return carry

    lax.fori_loop(0, shift_ref.shape[0] * (angles // LANES), tile, 0)


def interpolate(level, span, pieces, halves, slab):
    rows = jnp.concatenate([ref[part] for ref, _, _ in pieces for part in range(ref.shape[0])], 0)
    inter = jnp.dot(rows, halves[own_half(level)], preferred_element_type=f32).astype(bf16).astype(f32)
    at = 0
    for ref, near, far in pieces:
        place = pl.ds(pl.multiple_of(first_bin(span, near, far) + HALO, STEP), far - near)
        for part in range(ref.shape[0]):
            for j in range(inter.shape[1] // LANES):
                slab[part, j, place, :] = inter[at : at + far - near, j * LANES : (j + 1) * LANES]
            at += far - near
    place = pl.ds(pl.multiple_of(first_bin(span, -HALO, 0) + HALO, HALO), HALO)
    slab[:, :, place, :] = jnp.zeros((slab.shape[0], slab.shape[1], HALO, LANES), f32)


def pick(shift, bit, a, b):
    count = a.shape[0]
    mask = jnp.broadcast_to((shift >> bit & 1 == 1)[None], (count // ROWS, ROWS, LANES))
    return jnp.where(mask.reshape(count, LANES), a, b)


def shift_filter(slab, part, j, start, shift, taps, tmp, count):
    v = slab[part, j, pl.ds(start, count + 64), :]
    v = jnp.concatenate([pick(shift, 5, v[32 : count + 64], v[: count + 32]), v[count + 32 : count + 40]], 0)
    v = pick(shift, 4, v[16 : count + 40], v[: count + 24])
    v = pick(shift, 3, v[8 : count + 24], v[: count + 16])
    tmp[0, 0 : count + 16] = v
    v = pick(shift, 2, tmp[0, 4 : count + 20], v)
    tmp[1, 0 : count + 16] = v
    v = pick(shift, 1, tmp[1, 2 : count + 18], v)
    tmp[2, 0 : count + 16] = v
    total = None
    for t in range(taps.shape[0]):
        tap = jnp.broadcast_to(taps[t][None], (count // ROWS, ROWS, LANES)).reshape(count, LANES)
        term = tap * (v[:count] if t == 0 else tmp[2, t : t + count])
        total = term if total is None else total + term
    return total


def terms(slab, j, start, count, at, order, tables, tmp):
    shift_ref, taps_ref, phase_ref = tables
    shift, taps = shift_ref[at, order, j], taps_ref[at, order, j]
    re = shift_filter(slab, 0, j, start, shift, taps, tmp.at[0], count)
    im = shift_filter(slab, 1, j, start, shift, taps, tmp.at[1], count)
    c = phase_ref[at, order, 0, j, pl.ds(start, count), :]
    s = phase_ref[at, order, 1, j, pl.ds(start, count), :]
    return re * c - im * s, re * s + im * c


def own_kernel(level, at, span, stretches, near, far, *refs):
    pieces = [(ref, *stretch) for ref, stretch in zip(refs, stretches)]
    halves, *tables, acc, slab, tmp = refs[len(stretches) :]
    interpolate(level, span, pieces, halves, slab)
    start = first_bin(span, near, far)

    def tile(j, carry):
        acc[0, j], acc[1, j] = terms(slab, j, start, far - near, at, 0, tables, tmp)
        return carry

    lax.fori_loop(0, acc.shape[1], tile, 0)


def merge_kernel(level, at, span, stretches, near, far, held, final, *refs):
    pieces = [(ref, *stretch) for ref, stretch in zip(refs, stretches)]
    halves, acc, *tables = refs[len(stretches) : len(stretches) + 5]
    refs = refs[len(stretches) + 5 :]
    start, count = first_bin(span, near, far), far - near
    if final:
        ready, out, slab, tmp, merged = refs
        merged[:, pl.ds(first_bin(span, 0, near), near), :] = ready[...]
        into = start
    else:
        merged, slab, tmp = refs
        into = 0
    interpolate(level, span, pieces, halves, slab)
    acc_rows = pl.ds(pl.multiple_of(start - first_bin(span, *held), STEP), count)

    def tile(j, carry):
        lane = pl.ds(pl.multiple_of(j * LANES, LANES), LANES)
        for part, term in enumerate(terms(slab, j, start, count, at, 1, tables, tmp)):
            merged[part, pl.ds(into, count), lane] = (acc[part, j, acc_rows, :] + term).astype(bf16)
        return carry

    lax.fori_loop(0, acc.shape[1], tile, 0)
    if final:
        for part in range(out.shape[0]):
            out[part] = merged[part].T


def body(images, interp_matrix, offsets, tap_index, tap_table, phase_base, phase_slope):
    parts, angles, span = images.shape[1:]
    levels, roles, parent = offsets.shape
    tiles = angles // LANES
    taps_count = tap_table.shape[1]
    beyond = (span, span + HALO)
    edge_out = like((parts, HALO, angles), bf16)
    turned_outs = [like((parts, span, angles), bf16), edge_out]

    def work(count):
        return [pltpu.VMEM((parts, tiles, span + 2 * HALO, LANES), f32), pltpu.VMEM((parts, 3, count + 24, LANES), f32)]

    done = {}

    def step(name, *args):
        outs = run(name, *args, token=done.get(AFTER.get(name)), flops=WORK.get(name, 0))
        done[name] = outs[0]
        return outs

    def make_tables(name, first_level, count):
        outs = [
            like((count, roles, tiles, ROWS, LANES), jnp.int32),
            like((count, roles, tiles, taps_count + 1, ROWS, LANES), f32),
            like((count, roles, 2, tiles, span, LANES), f32),
        ]
        params = [offsets, tap_index, phase_base, phase_slope, tap_table.T]
        return step(name, functools.partial(tables_kernel, span, first_level), outs, params)

    def own(name, level, pieces, near=0, far=span):
        refs, stretches = zip(*pieces)
        at, tables = (0, first_tables) if level == 0 else (level - 1, later_tables)
        kernel = functools.partial(own_kernel, level, at, span, stretches, near, far)
        return step(name, kernel, [like((parts, tiles, far - near, LANES), f32)], [*refs, halves, *tables], work(far - near))[0]

    def merge(name, level, pieces, near, far, acc, held=(0, span), ready=None):
        refs, stretches = zip(*pieces)
        at, tables = (0, first_tables) if level == 0 else (level - 1, later_tables)
        final = ready is not None
        return step(
            name,
            functools.partial(merge_kernel, level, at, span, stretches, near, far, held, final),
            [like(images.shape[1:] if final else (parts, far - near, angles), bf16)],
            [*refs, halves, acc, *tables] + ([ready] if final else []),
            work(far - near) + ([pltpu.VMEM((parts, span, angles), bf16)] if final else []),
        )[0]

    def swap(value):
        return from_partner(value, "range", 1)

    received = from_partner(images[0], "aper", 1)
    current, edge = step("turn0", turn, turned_outs, [images[0]])
    own_edge = swap(edge)
    (halves,) = step("halves", halves_kernel, [like((2, angles, angles), bf16)], [interp_matrix])
    first_tables = make_tables("tables0", 0, 1)
    acc = own("own0", 0, [(current, (0, span)), (own_edge, beyond)])
    other, other_edge = step("turn1", turn, turned_outs, [received])
    other_edge = swap(other_edge)
    cut, middle, last = 96, 64, span - HALO
    outer = merge("m0o", 0, [(other, (0, span))], 0, cut, acc)

    other_outer = from_partner(outer, "aper", 2)
    later_tables = make_tables("tables12", 1, levels - 1)
    outer_acc = own("own1a", 1, [(outer, (0, cut))], 0, middle)
    inner = merge("m0i", 0, [(other, (0, span)), (other_edge, beyond)], cut, span, acc)
    other_inner = from_partner(inner, "aper", 2)
    own_edge = swap(step("edge1", edge_kernel, [edge_out], [inner])[0])
    new_outer = merge("m1o", 1, [(other_outer, (0, cut))], 0, middle, outer_acc, (0, middle))
    acc = own("own1b", 1, [(outer, (0, cut)), (inner, (cut, span)), (own_edge, beyond)], middle, span)
    other_edge = swap(step("copy1", edge_kernel, [edge_out], [other_inner])[0])
    pieces = [(other_outer, (0, cut)), (other_inner, (cut, span)), (other_edge, beyond)]
    edge = merge("m1e", 1, pieces, last, span, acc, (middle, span))
    inner = merge("m1i", 1, pieces, middle, last, acc, (middle, span))
    outer = new_outer

    other_outer = from_partner(outer, "aper", 4)
    other_edge = from_partner(edge, "aper", 4)
    other_inner = from_partner(inner, "aper", 4)
    acc = own("own2", 2, [(outer, (0, middle)), (inner, (middle, last)), (edge, (last, span)), (swap(edge), beyond)])
    pieces = [(other_outer, (0, middle)), (other_inner, (middle, last)), (other_edge, (last, span))]
    pieces += [(swap(step("copy2", copy_kernel, [edge_out], [other_edge])[0]), beyond)]
    first = middle - HALO
    ready = merge("f1", 2, [(other_outer, (0, middle))], 0, first, acc)
    return merge("f2", 2, pieces, first, span, acc, ready=ready)[None]


def solution(mesh):
    return jax.shard_map(
        body,
        mesh=mesh,
        in_specs=(P(("scene", "aper"), None, None, "range"), P(), P(), P(), P(), P(), P()),
        out_specs=P(("scene", "aper"), None, None, "range"),
        check_vma=False,
    )
```

```python
import functools

import jax
import jax.numpy as jnp
from jax import lax
from jax.experimental import pallas as pl
from jax.experimental.pallas import tpu as pltpu
from jax.sharding import PartitionSpec as P

HALO = 32
LANES = 128
ROWS = 8
STEP = 16
KERNEL_VMEM = 8 << 20
AFTER = {
    "m0i": "m0o",
    "own1b": "m1o",
    "copy2": "own2",
    "copy1": "m1o",
    "edge1": "m0i",
    "later": "m1e",
    "own1a": "tables12",
    "tables12": "own0",
    "turn1": "tables12",
}
WORK = {"m1o": 3000000000, "own1b": 3000000000, "m1i": 3000000000}
VMEM = pl.BlockSpec(memory_space=pltpu.VMEM)
like = jax.ShapeDtypeStruct
f32, bf16 = jnp.float32, jnp.bfloat16


def run(name, kernel, outs, args, scratch=(), aliases=None, token=None, flops=0):
    tokens = [] if token is None else [token]

    def without_token(*refs):
        kernel(*refs[: len(args)], *refs[len(args) + len(tokens) :])

    return pl.pallas_call(
        without_token,
        out_shape=outs,
        in_specs=[VMEM] * len(args) + [pl.BlockSpec(memory_space=pl.ANY)] * len(tokens),
        out_specs=[VMEM] * len(outs),
        scratch_shapes=scratch,
        input_output_aliases=aliases or {},
        name=name,
        compiler_params=pltpu.CompilerParams(vmem_limit_bytes=KERNEL_VMEM),
        cost_estimate=pl.CostEstimate(flops=flops, bytes_accessed=0, transcendentals=0),
    )(*args, *tokens)


def from_partner(value, axis, mask):
    pairs = [(source, source ^ mask) for source in range(lax.axis_size(axis))]
    return lax.ppermute(value, axis, pairs)


def first_bin(span, near, far):
    return pl.multiple_of(jnp.where(lax.axis_index("range") == 0, near, span - far), STEP)


def trimmed(stretch, near, far):
    return max(stretch[0], near - HALO), min(stretch[1], far + HALO)


def own_half(level):
    return lax.axis_index("aper") >> level & 1


def turn(image, turned, edge):
    span = turned.shape[1]
    for part in range(image.shape[0]):
        turned[part] = image[part].T
    edge[...] = turned[:, pl.ds(first_bin(span, span - HALO, span), HALO), :]


def halves_kernel(matrix, halves):
    angles = matrix.shape[1]
    for half in range(halves.shape[0]):
        halves[half] = matrix[half * angles : (half + 1) * angles, :].T


def edge_kernel(value, edge):
    width = value.shape[1]
    edge[...] = value[:, pl.ds(first_bin(width, width - HALO, width), HALO), :]


def copy_kernel(source, target):
    target[...] = source[...]


def tables_kernel(span, first_level, off, idx, base, slope, table, shift_ref, taps_ref, phase_ref):
    angles = off.shape[2] // 2
    start = lax.axis_index("range") * span
    taps_count = table.shape[0]
    columns = [jnp.broadcast_to(table[:, k : k + 1], (taps_count, LANES)) for k in range(table.shape[1])]

    def tile(at, carry):
        here, j = at // (angles // LANES), lax.rem(at, angles // LANES)
        level = here + first_level
        half = lax.axis_index("aper") >> level & 1
        lane = pl.ds(pl.multiple_of(half * angles + j * LANES, LANES), LANES)
        for order in range(2):
            role = half if order == 0 else 1 - half

            def row(ref):
                both = ref[level, :, lane]
                return jnp.broadcast_to(jnp.where(role == 0, both[0:1], both[1:2]), (ROWS, LANES))

            shift = row(off) + (HALO - 3)
            shift_ref[here, order, j] = shift
            which = row(idx)
            taps = jnp.zeros((taps_count, LANES), f32)
            for k, column in enumerate(columns):
                taps = jnp.where(which == k, column, taps)
            odd = shift & 1
            zero = jnp.zeros((ROWS, LANES), f32)
            rows = [jnp.broadcast_to(taps[t : t + 1], (ROWS, LANES)) for t in range(taps_count)]
            for t in range(taps_count + 1):
                even_tap = rows[t] if t < taps_count else zero
                odd_tap = rows[t - 1] if t > 0 else zero
                taps_ref[here, order, j, t] = jnp.where(odd == 1, odd_tap, even_tap)
            s = row(slope)
            ramp = lax.broadcasted_iota(jnp.int32, (ROWS, LANES), 0)
            near = row(base) + s * (ramp + start).astype(f32)
            c0, s0 = jnp.cos(near), jnp.sin(near)
            steps = span // ROWS
            far_at = lax.broadcasted_iota(jnp.int32, (steps, LANES), 0) * ROWS
            far = jnp.broadcast_to(s[0:1], (steps, LANES)) * far_at.astype(f32)
            c1, s1 = jnp.cos(far), jnp.sin(far)
            for u in range(steps):
                cu, su = c1[u : u + 1], s1[u : u + 1]
                bins = pl.ds(u * ROWS, ROWS)
                phase_ref[here, order, 0, j, bins, :] = c0 * cu - s0 * su
                phase_ref[here, order, 1, j, bins, :] = s0 * cu + c0 * su
        return carry

    lax.fori_loop(0, shift_ref.shape[0] * (angles // LANES), tile, 0)


def interpolate(level, span, pieces, halves, slab):
    rows = []
    for ref, held, used in pieces:
        skip = pl.multiple_of(first_bin(span, *used) - first_bin(span, *held), STEP)
        rows += [ref[part, pl.ds(skip, used[1] - used[0]), :] for part in range(ref.shape[0])]
    rows = jnp.concatenate(rows, 0)
    inter = jnp.dot(rows, halves[own_half(level)], preferred_element_type=f32).astype(bf16).astype(f32)
    at = 0
    for ref, _, (near, far) in pieces:
        place = pl.ds(pl.multiple_of(first_bin(span, near, far) + HALO, STEP), far - near)
        for part in range(ref.shape[0]):
            for j in range(inter.shape[1] // LANES):
                slab[part, j, place, :] = inter[at : at + far - near, j * LANES : (j + 1) * LANES]
            at += far - near
    place = pl.ds(pl.multiple_of(first_bin(span, -HALO, 0) + HALO, HALO), HALO)
    slab[:, :, place, :] = jnp.zeros((slab.shape[0], slab.shape[1], HALO, LANES), f32)


def pick(shift, bit, a, b):
    count = a.shape[0]
    mask = jnp.broadcast_to((shift >> bit & 1 == 1)[None], (count // ROWS, ROWS, LANES))
    return jnp.where(mask.reshape(count, LANES), a, b)


def shift_filter(slab, part, j, start, shift, taps, tmp, count):
    v = slab[part, j, pl.ds(start, count + 64), :]
    v = jnp.concatenate([pick(shift, 5, v[32 : count + 64], v[: count + 32]), v[count + 32 : count + 40]], 0)
    v = pick(shift, 4, v[16 : count + 40], v[: count + 24])
    v = pick(shift, 3, v[8 : count + 24], v[: count + 16])
    tmp[0, 0 : count + 16] = v
    v = pick(shift, 2, tmp[0, 4 : count + 20], v)
    tmp[1, 0 : count + 16] = v
    v = pick(shift, 1, tmp[1, 2 : count + 18], v)
    tmp[2, 0 : count + 16] = v
    total = None
    for t in range(taps.shape[0]):
        tap = jnp.broadcast_to(taps[t][None], (count // ROWS, ROWS, LANES)).reshape(count, LANES)
        term = tap * (v[:count] if t == 0 else tmp[2, t : t + count])
        total = term if total is None else total + term
    return total


def terms(slab, j, start, count, at, order, tables, tmp):
    shift_ref, taps_ref, phase_ref = tables
    shift, taps = shift_ref[at, order, j], taps_ref[at, order, j]
    re = shift_filter(slab, 0, j, start, shift, taps, tmp.at[0], count)
    im = shift_filter(slab, 1, j, start, shift, taps, tmp.at[1], count)
    c = phase_ref[at, order, 0, j, pl.ds(start, count), :]
    s = phase_ref[at, order, 1, j, pl.ds(start, count), :]
    return re * c - im * s, re * s + im * c


def own_kernel(level, at, span, stretches, near, far, *refs):
    pieces = [(ref, held, trimmed(held, near, far)) for ref, held in zip(refs, stretches)]
    halves, *tables, acc, slab, tmp = refs[len(stretches) :]
    interpolate(level, span, pieces, halves, slab)
    start = first_bin(span, near, far)

    def tile(j, carry):
        acc[0, j], acc[1, j] = terms(slab, j, start, far - near, at, 0, tables, tmp)
        return carry

    lax.fori_loop(0, acc.shape[1], tile, 0)


def merge_kernel(level, at, span, stretches, near, far, held, mode, *refs):
    pieces = [(ref, got, got if mode == "early" else trimmed(got, near, far)) for ref, got in zip(refs, stretches)]
    halves, acc, *tables = refs[len(stretches) : len(stretches) + 5]
    refs = refs[len(stretches) + 5 :]
    start, count = first_bin(span, near, far), far - near
    if mode == "last":
        ready, _, out, slab, tmp, merged = refs
        merged[:, pl.ds(first_bin(span, 0, near), near), :] = ready[...]
        into = start
    else:
        merged, slab, tmp = refs
        into = 0
    interpolate(level, span, pieces, halves, slab)
    acc_rows = pl.ds(pl.multiple_of(start - first_bin(span, *held), STEP), count)

    def tile(j, carry):
        lane = pl.ds(pl.multiple_of(j * LANES, LANES), LANES)
        for part, term in enumerate(terms(slab, j, start, count, at, 1, tables, tmp)):
            merged[part, pl.ds(into, count), lane] = (acc[part, j, acc_rows, :] + term).astype(bf16)
        return carry

    lax.fori_loop(0, acc.shape[1], tile, 0)
    if mode == "last":
        for part in range(out.shape[0]):
            out[part] = merged[part].T


def body(images, interp_matrix, offsets, tap_index, tap_table, phase_base, phase_slope):
    parts, angles, span = images.shape[1:]
    levels, roles, parent = offsets.shape
    tiles = angles // LANES
    taps_count = tap_table.shape[1]
    beyond = (span, span + HALO)
    edge_out = like((parts, HALO, angles), bf16)
    turned_outs = [like((parts, span, angles), bf16), edge_out]

    def work(count):
        return [pltpu.VMEM((parts, tiles, span + 2 * HALO, LANES), f32), pltpu.VMEM((parts, 3, count + 24, LANES), f32)]

    done = {}

    def step(name, *args):
        outs = run(name, *args, token=done.get(AFTER.get(name)), flops=WORK.get(name, 0))
        done[name] = outs[0]
        return outs

    def make_tables(name, first_level, count):
        outs = [
            like((count, roles, tiles, ROWS, LANES), jnp.int32),
            like((count, roles, tiles, taps_count + 1, ROWS, LANES), f32),
            like((count, roles, 2, tiles, span, LANES), f32),
        ]
        params = [offsets, tap_index, phase_base, phase_slope, tap_table.T]
        return step(name, functools.partial(tables_kernel, span, first_level), outs, params)

    def own(name, level, pieces, near=0, far=span):
        refs, stretches = zip(*pieces)
        at, tables = (0, first_tables) if level == 0 else (level - 1, later_tables)
        kernel = functools.partial(own_kernel, level, at, span, stretches, near, far)
        return step(name, kernel, [like((parts, tiles, far - near, LANES), f32)], [*refs, halves, *tables], work(far - near))[0]

    def merge(name, level, pieces, near, far, acc, held=(0, span), mode="", ready=()):
        refs, stretches = zip(*pieces)
        at, tables = (0, first_tables) if level == 0 else (level - 1, later_tables)
        args = [*refs, halves, acc, *tables, *ready]
        outs = [like(images.shape[1:] if mode == "last" else (parts, far - near, angles), bf16)]
        slab, tmp = work(far - near)
        if mode:
            outs.append(like((parts, tiles, span + 2 * HALO, LANES), f32))
        scratch = ([] if mode else [slab]) + [tmp]
        if mode == "last":
            scratch.append(pltpu.VMEM((parts, span, angles), bf16))
        kernel = functools.partial(merge_kernel, level, at, span, stretches, near, far, held, mode)
        result = step(name, kernel, outs, args, scratch, {len(args) - 1: 1} if mode == "last" else None)
        return result if mode == "early" else result[0]

    def swap(value):
        return from_partner(value, "range", 1)

    received = from_partner(images[0], "aper", 1)
    current, edge = step("turn0", turn, turned_outs, [images[0]])
    own_edge = swap(edge)
    (halves,) = step("halves", halves_kernel, [like((2, angles, angles), bf16)], [interp_matrix])
    first_tables = make_tables("tables0", 0, 1)
    acc = own("own0", 0, [(current, (0, span)), (own_edge, beyond)])
    other, other_edge = step("turn1", turn, turned_outs, [received])
    other_edge = swap(other_edge)
    cut, middle, last = 96, 64, span - HALO
    outer = merge("m0o", 0, [(other, (0, span))], 0, cut, acc)

    other_outer = from_partner(outer, "aper", 2)
    later_tables = make_tables("tables12", 1, levels - 1)
    outer_acc = own("own1a", 1, [(outer, (0, cut))], 0, middle)
    inner = merge("m0i", 0, [(other, (0, span)), (other_edge, beyond)], cut, span, acc)
    other_inner = from_partner(inner, "aper", 2)
    own_edge = swap(step("edge1", edge_kernel, [edge_out], [inner])[0])
    new_outer = merge("m1o", 1, [(other_outer, (0, cut))], 0, middle, outer_acc, (0, middle))
    acc = own("own1b", 1, [(outer, (0, cut)), (inner, (cut, span)), (own_edge, beyond)], middle, span)
    other_edge = swap(step("copy1", edge_kernel, [edge_out], [other_inner])[0])
    pieces = [(other_outer, (0, cut)), (other_inner, (cut, span)), (other_edge, beyond)]
    inner = merge("m1i", 1, pieces[:2], middle, last, acc, (middle, span))
    edge = merge("m1e", 1, pieces, last, span, acc, (middle, span))
    (inner,) = step("later", copy_kernel, [like(inner.shape, bf16)], [inner])
    outer = new_outer

    other_outer = from_partner(outer, "aper", 4)
    other_edge = from_partner(edge, "aper", 4)
    other_inner = from_partner(inner, "aper", 4)
    acc = own("own2", 2, [(outer, (0, middle)), (inner, (middle, last)), (edge, (last, span)), (swap(edge), beyond)])
    beyond_edge = swap(step("copy2", copy_kernel, [edge_out], [other_edge])[0])
    first = middle - HALO
    ready = merge("f1", 2, [(other_outer, (0, middle)), (other_edge, (last, span))], 0, first, acc, mode="early")
    pieces = [(other_inner, (middle, last)), (beyond_edge, beyond)]
    return merge("f2", 2, pieces, first, span, acc, mode="last", ready=ready)[None]


def solution(mesh):
    return jax.shard_map(
        body,
        mesh=mesh,
        in_specs=(P(("scene", "aper"), None, None, "range"), P(), P(), P(), P(), P(), P()),
        out_specs=P(("scene", "aper"), None, None, "range"),
        check_vma=False,
    )
```
